32 devices in a mesh: groups: 1, tile: 32 (over z, y, x, core).
Axes of the slice: x: 2, y: 2, z: 4, core: 2. Of those that a mesh axis runs over, the one named last changes fastest.
Arguments:
- fields: bfloat16 [96, 512, 1024], P('groups', 'tile'), may hold values from -6 to 6
- kernel: float32 [9, 1024], replicated, may hold values from -2 to 2
- norm_gain: float32 [1024], replicated, may hold values from 0.5 to 2
- land_bias: float32 [1024], replicated, may hold values from -6 to 6
- w_in: bfloat16 [1024, 1024], replicated, may hold values from -0.1875 to 0.1875
- w_out: bfloat16 [1024, 1024], replicated, may hold values from -0.1875 to 0.1875
- land_mask: int32 [96, 512], P('groups', 'tile'), may hold values 0 or 1
- cotangent: bfloat16 [96, 512, 1024], P('groups', 'tile'), may hold values from -6 to 6
Outputs:
- grad_fields: bfloat16 [96, 512, 1024], P('groups', 'tile')
- grad_w_in: float32 [1024, 1024], P('groups')
- grad_w_out: float32 [1024, 1024], P('groups')
- grad_kernel: float32 [9, 1024], P('groups')
- grad_gain: float32 [1024], P('groups')
- grad_land: float32 [1024], P('groups')
The draws below stay inside these ranges and needn't reach their ends.
All inputs are finite; a program needn't handle non-finite values. No bound on the sum of `land_mask` on one device may be relied on, other than what follows from the above.
Results may differ from the reference program's by a relative error of at most 0.0075.
Values may be sent and summed in bfloat16 or wider, within the bound.
A program may use at most 128 MiB of HBM per device.

```python
import math
import jax
import jax.numpy as jnp
from jax import lax

C = 1024
LAT = 96
LON = 512


def with_ends(array, stream_key, smallest, high):
    shape = array.shape
    spot = [jax.random.randint(jax.random.fold_in(stream_key, axis), (), 0, shape[axis]) for axis in range(len(shape))]
    array = array.at[tuple(spot)].set(smallest)
    longest = shape.index(max(shape))
    spot[longest] = (spot[longest] + 1) % shape[longest]
    return array.at[tuple(spot)].set(high)


def level_of(rng, extent, cuts, low, largest):
    factor_of = 1.0
    for position, blocks in cuts:
        steps = jax.random.uniform(jax.random.fold_in(jax.random.fold_in(rng, 6), position), (blocks,), jnp.float32, low / len(cuts), largest / len(cuts))
        factor_of = factor_of * jnp.repeat(jnp.exp(steps), extent[position] // blocks).reshape((-1,) + (1,) * (len(extent) - 1 - position))
    return factor_of


def normal_values(own_key, extent, deviation, limit, pieces=(), kind=jnp.bfloat16):
    array = jax.random.normal(own_key, extent, jnp.float32) * deviation
    if len(pieces) > 0:
        array = level_of(own_key, extent, pieces, -0.22, 0.18) * array
    return jnp.clip(array, min=-limit, max=limit).astype(kind)


def setup_inputs(seed: int = 0, part: int = 0) -> dict:
    streams_of = jax.random.split(jax.random.key(seed), 9)
    part_keys = jax.random.split(jax.random.fold_in(streams_of[8], part), 9)
    return {
        "fields": normal_values(part_keys[0], (LAT, LON, C), 1.0, 6.0, ((1, 32),)),
        "kernel": normal_values(streams_of[1], (9, C), 9 ** -0.5, 2.0, (), jnp.float32),
        "norm_gain": jnp.clip(jnp.exp(jax.random.uniform(streams_of[2], (C,), jnp.float32, math.log(0.5), math.log(2.0))), 0.5, 2.0),
        "land_bias": normal_values(streams_of[3], (C,), 1.0, 6.0, (), jnp.float32),
        "w_in": normal_values(streams_of[4], (C, C), C ** -0.5, 0.1875),
        "w_out": normal_values(streams_of[5], (C, C), C ** -0.5, 0.1875),
        "land_mask": with_ends((jax.random.randint(part_keys[6], (LAT, LON), 0, 10) < 3).astype(jnp.int32), jax.random.fold_in(part_keys[6], 1), 0, 1),
        "cotangent": normal_values(part_keys[7], (LAT, LON, C), 1.0, 6.0, ((1, 32),)),
    }


EPS = 1e-06
INV_ROOT_TWO = 0.7071067811865476
INV_ROOT_TWO_PI = 0.3989422804014327

def extend(field):
    rolled = jnp.roll(field, LON // 2, axis=1)
    wide = jnp.concatenate([field[:, -1:], field, field[:, :1]], axis=1)
    turned = jnp.concatenate([rolled[:, -1:], rolled, rolled[:, :1]], axis=1)
    return jnp.concatenate([turned[:1], wide, turned[-1:]], axis=0)

def depthwise(field, kernel):
    padded = extend(field)
    total = jnp.zeros(field.shape, jnp.float32)
    for row in range(3):
        for col in range(3):
            total = total + kernel[3 * row + col] * padded[row:row + LAT, col:col + LON]
    return total

def reference(fields, kernel, norm_gain, land_bias, w_in, w_out, land_mask, cotangent):
    as_float = fields.astype(jnp.float32)
    land = land_mask.astype(jnp.float32)[:, :, None]
    depth = depthwise(as_float, kernel) + land * land_bias
    scale = lax.rsqrt(lax.optimization_barrier(jnp.mean(depth * depth, axis=-1, keepdims=True)) + EPS)
    normed = (depth * scale * norm_gain).astype(jnp.bfloat16).reshape(-1, C)
    pre = jnp.dot(normed, w_in, preferred_element_type=jnp.float32)
    cdf = 0.5 * (1.0 + lax.erf(pre * INV_ROOT_TWO))
    hidden = (pre * cdf).astype(jnp.bfloat16)
    upstream = cotangent.reshape(-1, C)
    grad_w_out = jnp.dot(hidden.T, upstream, preferred_element_type=jnp.float32)
    g_hidden = jnp.dot(upstream, w_out.T, preferred_element_type=jnp.float32)
    slope = cdf + pre * jnp.exp(-0.5 * pre * pre) * INV_ROOT_TWO_PI
    g_pre = (g_hidden * slope).astype(jnp.bfloat16)
    grad_w_in = jnp.dot(normed.T, g_pre, preferred_element_type=jnp.float32)
    g_normed = jnp.dot(g_pre, w_in.T, preferred_element_type=jnp.float32).reshape(LAT, LON, C)
    grad_gain = lax.optimization_barrier(jnp.sum(g_normed * depth * scale, axis=(0, 1)))
    weighted = g_normed * norm_gain
    inner = lax.optimization_barrier(jnp.mean(weighted * depth, axis=-1, keepdims=True))
    g_depth = (scale * weighted - depth * scale * scale * scale * inner).astype(jnp.bfloat16)
    g_float = g_depth.astype(jnp.float32)
    _, pull = jax.vjp(depthwise, as_float, kernel)
    g_conv, grad_kernel = pull(g_float)
    grad_land = lax.optimization_barrier(jnp.sum(g_float * land, axis=(0, 1)))
    grad_fields = (g_conv + cotangent.astype(jnp.float32)).astype(jnp.bfloat16)
    return (grad_fields, grad_w_in, grad_w_out, grad_kernel, grad_gain, grad_land)
```

```python
import functools

import jax
import jax.numpy as jnp
from jax import lax
from jax.experimental import pallas as pl
from jax.experimental.pallas import tpu as pltpu
from jax.sharding import PartitionSpec as P

EPS = 1e-06
INV_ROOT_TWO = 0.7071067811865476
INV_ROOT_TWO_PI = 0.3989422804014327
F32 = jnp.float32
BF16 = jnp.bfloat16
LANES = 256
NT = (((1,), (1,)), ((), ()))
TN = (((0,), (0,)), ((), ()))


def block_kernel(
    count, fields_hbm, cot_hbm, w_in_hbm, w_out_hbm, taps, gain, bias, land,
    out_hbm, gw_hbm, small_out,
    F, COT, WI, WO, D, NRM, GH, HID, GP, GX, PRE, SC, G, RB, RP, A,
    COL, HX, EDGE, CS, CR, KS, KR, GA, LA, SS, SR,
    load_sem, halo_send, halo_recv, rs_send, rs_recv, ag_send, ag_recv, sm_send, sm_recv,
):
    rows, cols, chans = COT.shape
    me = lax.axis_index("tile")
    bits = count.bit_length() - 1
    half = count // 2
    right = (me + 1) % count
    left = (me + count - 1) % count
    across = (me + half) % count
    across_right = (me + half + 1) % count
    across_left = (me + half - 1) % count

    def bit_of(b):
        return (me // (1 << b)) % 2

    def peer(b):
        return me + (1 - 2 * bit_of(b)) * (1 << b)

    def remote(src, dst, send, recv, target):
        return pltpu.make_async_remote_copy(
            src_ref=src, dst_ref=dst, send_sem=send, recv_sem=recv,
            device_id={"tile": target}, device_id_type=pl.DeviceIdType.MESH,
        )

    load_f = pltpu.make_async_copy(fields_hbm, F.at[pl.ds(1, rows)], load_sem.at[0])
    load_c = pltpu.make_async_copy(cot_hbm, COT, load_sem.at[1])
    load_o = pltpu.make_async_copy(w_out_hbm, WO, load_sem.at[2])
    load_i = pltpu.make_async_copy(w_in_hbm, WI, load_sem.at[3])
    load_f.start()
    load_c.start()
    load_o.start()
    load_i.start()

    friends = [right, left, across, across_right, across_left] + [peer(b) for b in range(bits - 1)]
    barrier = pltpu.get_barrier_semaphore()
    for friend in friends:
        pl.semaphore_signal(barrier, inc=1, device_id={"tile": friend}, device_id_type=pl.DeviceIdType.MESH)
    pl.semaphore_wait(barrier, len(friends))

    lane_chunks = [pl.ds(c * LANES, LANES) for c in range(chans // LANES)]
    spot = lax.broadcasted_iota(jnp.int32, (cols, LANES), 0)
    first = spot == 0
    last = spot == cols - 1

    def send_halo(ext, base):
        copies = [
            remote(ext.at[1], ext.at[0], halo_send.at[base], halo_recv.at[base], across),
            remote(ext.at[rows], ext.at[rows + 1], halo_send.at[base + 1], halo_recv.at[base + 1], across),
        ]
        slot = 0 if base == 0 else 2
        for copy in copies:
            copy.start()
        for side in range(2):
            def rounded(t, _):
                at = pl.ds(pl.multiple_of(t * 16, 16), 16)
                CS[slot + side, at, :] = COL[side, at, :].astype(BF16)
                return 0
            lax.fori_loop(0, rows // 16, rounded, 0)
            ends = jnp.concatenate([COL[side, 0:8, :], COL[side, rows - 8 : rows, :]], axis=0)
            KS[slot + side] = ends.astype(BF16)
        more = [
            remote(CS.at[slot + 1], CR.at[slot], halo_send.at[base + 2], halo_recv.at[base + 2], right),
            remote(CS.at[slot], CR.at[slot + 1], halo_send.at[base + 3], halo_recv.at[base + 3], left),
            remote(KS.at[slot + 1], KR.at[slot], halo_send.at[base + 4], halo_recv.at[base + 4], across_right),
            remote(KS.at[slot], KR.at[slot + 1], halo_send.at[base + 5], halo_recv.at[base + 5], across_left),
        ]
        for copy in more:
            copy.start()
        return copies + more

    def widen_halo(slot):
        for side in range(2):
            def opened(t, _):
                at = pl.ds(pl.multiple_of(t * 16, 16), 16)
                HX[side, pl.ds(pl.multiple_of(8 + t * 16, 8), 16), :] = CR[slot + side, at, :].astype(F32)
                return 0
            lax.fori_loop(0, rows // 16, opened, 0)
            ends = KR[slot + side].astype(F32)
            HX[side, 7:8, :] = ends[0:1]
            HX[side, 8 + rows : 9 + rows, :] = ends[15:16]

    load_f.wait()

    def take_columns(i, _):
        row = F[i + 1].astype(F32)
        COL[0, pl.ds(i, 1), :] = row[0:1]
        COL[1, pl.ds(i, 1), :] = row[cols - 1 : cols]
        return 0
    lax.fori_loop(0, rows, take_columns, 0)
    halo = send_halo(F, 0)

    load_c.wait()
    load_o.wait()
    load_i.wait()
    step = 16
    blocks = rows // step

    def hidden_grad(k, _):
        at = pl.ds(k * step, step)
        up = COT[at].reshape(step * cols, chans)
        for lanes in lane_chunks:
            GH[at, :, lanes] = lax.dot_general(
                up, WO[lanes, :], NT, preferred_element_type=F32
            ).reshape(step, cols, LANES)
        return 0
    lax.fori_loop(0, blocks, hidden_grad, 0)

    for copy in halo:
        copy.wait()
    widen_halo(0)
    for lanes in lane_chunks:
        for side in range(2):
            total = taps[2 * side : 2 * side + 1, lanes] * HX[side, 7 : 7 + rows, lanes]
            for a in range(1, 3):
                t = 3 * a + 2 * side
                total = total + taps[t : t + 1, lanes] * HX[side, 7 + a : 7 + a + rows, lanes]
            EDGE[side, :, lanes] = total

    def forward(k, _):
        def norm_row(q, _):
            i = k * step + q
            squares = jnp.zeros((cols, 128), F32)
            ground = land[i]
            for lanes in lane_chunks:
                window = [F[i + a, :, lanes].astype(F32) for a in range(3)]
                sums = []
                for b in range(3):
                    s = taps[b : b + 1, lanes] * window[0]
                    for a in range(1, 3):
                        s = s + taps[3 * a + b : 3 * a + b + 1, lanes] * window[a]
                    sums.append(s)
                depth = sums[1]
                depth = depth + jnp.where(first, EDGE[0, pl.ds(i, 1), lanes], pltpu.roll(sums[0], 1, 0))
                depth = depth + jnp.where(last, EDGE[1, pl.ds(i, 1), lanes], pltpu.roll(sums[2], cols - 1, 0))
                depth = depth + jnp.concatenate([ground] * (LANES // 128), axis=1) * bias[0:1, lanes]
                D[i, :, lanes] = depth
                for part in range(LANES // 128):
                    piece = depth[:, part * 128 : (part + 1) * 128]
                    squares = squares + piece * piece
            mean = jnp.sum(squares, axis=1, keepdims=True) * (1.0 / chans)
            scale = lax.rsqrt(mean + EPS)
            SC[i] = jnp.broadcast_to(scale, (cols, 128))
            for lanes in lane_chunks:
                NRM[i, :, lanes] = (D[i, :, lanes] * scale * gain[0:1, lanes]).astype(BF16)
            return 0
        lax.fori_loop(0, step, norm_row, 0)
        normed = NRM[pl.ds(k * step, step)].reshape(step * cols, chans)
        for lanes in lane_chunks:
            PRE[:, :, lanes] = jnp.dot(
                normed, WI[:, lanes], preferred_element_type=F32
            ).reshape(step, cols, LANES)

        def gelu_row(q, _):
            i = k * step + q
            for lanes in lane_chunks:
                pre = PRE[q, :, lanes]
                cdf = 0.5 * (1.0 + lax.erf(pre * INV_ROOT_TWO))
                slope = cdf + pre * jnp.exp(-0.5 * pre * pre) * INV_ROOT_TWO_PI
                HID[i, :, lanes] = (pre * cdf).astype(BF16)
                GP[i, :, lanes] = (GH[i, :, lanes] * slope).astype(BF16)
            return 0
        lax.fori_loop(0, step, gelu_row, 0)
        return 0
    lax.fori_loop(0, blocks, forward, 0)

    core = bit_of(0)
    mid = chans // 2
    keep0 = pl.multiple_of(core * mid, mid)
    send0 = pl.multiple_of((1 - core) * mid, mid)

    def weight_grad(w, lhs, rhs, base):
        def chunk(t, _):
            at = pl.ds(pl.multiple_of(base + t * LANES, LANES), LANES)
            left_side = lhs[:, :, at].reshape(rows * cols, LANES)
            for lanes in lane_chunks:
                right_side = rhs[:, :, lanes].reshape(rows * cols, LANES)
                G[w, at, lanes] = lax.dot_general(
                    left_side, right_side, TN, preferred_element_type=F32
                ).astype(BF16)
            return 0
        lax.fori_loop(0, mid // LANES, chunk, 0)

    def swap_core(w):
        copy = remote(G.at[w, pl.ds(send0, mid)], RB.at[w], rs_send.at[w], rs_recv.at[w], peer(0))
        copy.start()
        return copy

    def fold(w, base, size, source, offset):
        def add(t, _):
            at = pl.ds(pl.multiple_of(base + t * 16, 16), 16)
            come = source[pl.ds(pl.multiple_of(offset + t * 16, 16), 16), :]
            G[w, at, :] = (G[w, at, :].astype(F32) + come.astype(F32)).astype(BF16)
            return 0
        lax.fori_loop(0, size // 16, add, 0)

    middle = list(range(1, bits - 1))
    pieces = mid // 2
    orders = []
    bases = []
    for p in range(4):
        turn = p % len(middle)
        orders.append(middle[turn:] + middle[:turn] + [bits - 1])
        bases.append([keep0 + (p % 2) * pieces])
    stages = bits - 1
    offsets = [pieces - (pieces >> s) for s in range(stages)]

    def rs_start(p, s):
        size = pieces >> (s + 1)
        b = orders[p][s]
        base = bases[p][s]
        away = pl.multiple_of(base + (1 - bit_of(b)) * size, 16)
        bases[p].append(base + bit_of(b) * size)
        n = 2 + p * stages + s
        copy = remote(
            G.at[p // 2, pl.ds(away, size)], RP.at[p, pl.ds(offsets[s], size)],
            rs_send.at[n], rs_recv.at[n], peer(b),
        )
        copy.start()
        return copy

    def rs_finish(copy, p, s):
        copy.wait()
        fold(p // 2, bases[p][s + 1], pieces >> (s + 1), RP.at[p], offsets[s])

    def ag_start(p, s):
        size = pieces >> (s + 1)
        at = pl.ds(pl.multiple_of(bases[p][s + 1], 16), size)
        b = orders[p][s] if s >= 0 else 0
        n = p * bits + s + 1
        copy = remote(A.at[p // 2, at], A.at[p // 2, at], ag_send.at[n], ag_recv.at[n], peer(b))
        copy.start()
        return copy

    flight = {}

    def advance(p):
        state, copy = flight[p]
        if state[0] == "rs":
            s = state[1]
            rs_finish(copy, p, s)
            if s + 1 < stages:
                flight[p] = (("rs", s + 1), rs_start(p, s + 1))
            else:
                at = pl.ds(pl.multiple_of(bases[p][stages], 16), pieces >> stages)
                A[p // 2, at, :] = G[p // 2, at, :]
                flight[p] = (("ag", stages - 1), ag_start(p, stages - 1))
        elif state[0] == "ag":
            s = state[1]
            copy.wait()
            if s >= 0:
                flight[p] = (("ag", s - 1), ag_start(p, s - 1))
            else:
                flight[p] = (("done",), None)

    weight_grad(0, HID, COT, send0)
    core0 = swap_core(0)
    weight_grad(0, HID, COT, keep0)
    core0.wait()
    fold(0, keep0, mid, RB.at[0], 0)
    for p in (0, 1):
        flight[p] = (("rs", 0), rs_start(p, 0))
    weight_grad(1, NRM, GP, send0)
    core1 = swap_core(1)
    weight_grad(1, NRM, GP, keep0)
    core1.wait()
    fold(1, keep0, mid, RB.at[1], 0)
    for p in (2, 3):
        flight[p] = (("rs", 0), rs_start(p, 0))
    for p in (0, 1):
        advance(p)

    GA[...] = jnp.zeros_like(GA)
    LA[...] = jnp.zeros_like(LA)

    def backward(k, _):
        at = pl.ds(k * step, step)
        g_pre = GP[at].reshape(step * cols, chans)
        for lanes in lane_chunks:
            GH[at, :, lanes] = lax.dot_general(
                g_pre, WI[lanes, :], NT, preferred_element_type=F32
            ).reshape(step, cols, LANES)

        def norm_row(q, _):
            i = k * step + q
            scale = SC[i]
            wide = jnp.concatenate([scale] * (LANES // 128), axis=1)
            ground = jnp.concatenate([land[i]] * (LANES // 128), axis=1)
            inner = jnp.zeros((cols, 128), F32)
            for lanes in lane_chunks:
                g = GH[i, :, lanes]
                product = g * D[i, :, lanes]
                GA[:, lanes] = GA[:, lanes] + product * wide
                weighted = product * gain[0:1, lanes]
                for part in range(LANES // 128):
                    inner = inner + weighted[:, part * 128 : (part + 1) * 128]
            mean = jnp.sum(inner, axis=1, keepdims=True) * (1.0 / chans)
            cube = scale * scale * scale * mean
            cube = jnp.concatenate([cube] * (LANES // 128), axis=1)
            for lanes in lane_chunks:
                g = wide * (GH[i, :, lanes] * gain[0:1, lanes]) - D[i, :, lanes] * cube
                rounded = g.astype(BF16)
                GX[i + 1, :, lanes] = rounded
                g = rounded.astype(F32)
                LA[:, lanes] = LA[:, lanes] + g * ground
                COL[0, pl.ds(i, 1), lanes] = g[0:1]
                COL[1, pl.ds(i, 1), lanes] = g[cols - 1 : cols]
            return 0
        lax.fori_loop(0, step, norm_row, 0)
        return 0

    cut = blocks // 2
    lax.fori_loop(0, cut, backward, 0)
    for p in range(4):
        advance(p)
    lax.fori_loop(cut, blocks, backward, 0)
    g_halo = send_halo(GX, 6)
    for p in range(4):
        advance(p)

    zero = jnp.zeros((8, LANES), F32)
    for c, lanes in enumerate(lane_chunks):
        def tap_row(i, sums):
            g = GX[i + 1, :, lanes].astype(F32)
            sides = [
                jnp.where(last, 0.0, pltpu.roll(g, cols - 1, 0)),
                g,
                jnp.where(first, 0.0, pltpu.roll(g, 1, 0)),
            ]
            new = []
            for a in range(3):
                row = F[i + a, :, lanes].astype(F32)
                for b in range(3):
                    product = sides[b] * row
                    piece = product[0:8]
                    for top in range(8, cols, 8):
                        piece = piece + product[top : top + 8]
                    new.append(sums[3 * a + b] + piece)
            return tuple(new)
        sums = list(lax.fori_loop(0, rows, tap_row, (zero,) * 9))
        lines = []
        for a in range(3):
            for b in range(3):
                line = jnp.sum(sums[3 * a + b], axis=0, keepdims=True)
                if b != 1:
                    side = b // 2
                    line = line + jnp.sum(
                        COL[side, :, lanes] * HX[side, 7 + a : 7 + a + rows, lanes], axis=0, keepdims=True
                    )
                lines.append(line)
        lines.append(jnp.sum(GA[:, lanes], axis=0, keepdims=True))
        lines.append(jnp.sum(LA[:, lanes], axis=0, keepdims=True))
        lines.append(jnp.zeros((5, LANES), F32))
        SS[0, :, lanes] = jnp.concatenate(lines, axis=0)
        advance(c % 4)

    def small_start(b):
        copy = remote(SS.at[b], SR.at[b], sm_send.at[b], sm_recv.at[b], peer(b))
        copy.start()
        return copy

    def small_finish(copy, b):
        copy.wait()
        SS[b + 1] = SS[b] + SR[b]

    small = small_start(0)
    for copy in g_halo:
        copy.wait()
    widen_halo(2)
    for lanes in lane_chunks:
        for side in range(2):
            north = HX[side, 7:8, lanes]
            south = HX[side, 8 + rows : 9 + rows, lanes]
            near = 2 - 2 * side
            middle_rows = taps[3 + near : 4 + near, lanes] * HX[side, 8 : 8 + rows, lanes]
            above = taps[6 + near : 7 + near, lanes] * HX[side, 7 : 7 + rows, lanes]
            below = taps[near : near + 1, lanes] * HX[side, 9 : 9 + rows, lanes]
            line = lax.broadcasted_iota(jnp.int32, (rows, LANES), 0)
            above = jnp.where(line == 0, taps[near : near + 1, lanes] * north, above)
            below = jnp.where(line == rows - 1, taps[6 + near : 7 + near, lanes] * south, below)
            EDGE[side, :, lanes] = middle_rows + above + below

    def spread_row(i, top, bottom):
        for lanes in lane_chunks:
            above = GX[i, :, lanes].astype(F32)
            here = GX[i + 1, :, lanes].astype(F32)
            below = GX[i + 2, :, lanes].astype(F32)
            sums = []
            for b in range(3):
                s = taps[3 * top + b : 3 * top + b + 1, lanes] * above
                s = s + taps[3 + b : 4 + b, lanes] * here
                s = s + taps[3 * bottom + b : 3 * bottom + b + 1, lanes] * below
                sums.append(s)
            total = sums[1] + COT[i, :, lanes].astype(F32)
            total = total + jnp.where(last, EDGE[1, pl.ds(i, 1), lanes], pltpu.roll(sums[0], cols - 1, 0))
            total = total + jnp.where(first, EDGE[0, pl.ds(i, 1), lanes], pltpu.roll(sums[2], 1, 0))
            HID[i, :, lanes] = total.astype(BF16)

    def spread(i, _):
        spread_row(i, 2, 0)
        return 0

    spread_row(0, 0, 0)
    spread_row(rows - 1, 2, 2)
    legs = bits
    edges = [1 + (rows - 2) * t // legs for t in range(legs + 1)]
    for t in range(legs):
        lax.fori_loop(edges[t], edges[t + 1], spread, 0)
        small_finish(small, t)
        if t + 1 < bits:
            small = small_start(t + 1)
        for p in range(4):
            advance(p)
    store = pltpu.make_async_copy(HID, out_hbm, load_sem.at[0])
    store.start()
    for _ in range(2 * bits):
        for p in range(4):
            advance(p)
    small_out[...] = SS[bits]
    save = pltpu.make_async_copy(A, gw_hbm, load_sem.at[1])
    save.start()
    store.wait()
    save.wait()


def body(fields, kernel, norm_gain, land_bias, w_in, w_out, land_mask, cotangent):
    rows, cols, chans = fields.shape
    count = lax.axis_size("tile")
    bits = count.bit_length() - 1
    land = jnp.broadcast_to(land_mask.astype(F32)[:, :, None], (rows, cols, 128))
    vm = pltpu.VMEM
    grid3 = (rows, cols, chans)
    dma = pltpu.SemaphoreType.DMA
    anywhere = pl.BlockSpec(memory_space=pl.ANY)
    inside = pl.BlockSpec(memory_space=pltpu.VMEM)
    pieces = chans // 4
    out, gw, small = pl.pallas_call(
        functools.partial(block_kernel, count),
        out_shape=(
            jax.ShapeDtypeStruct(grid3, BF16),
            jax.ShapeDtypeStruct((2, chans, chans), BF16),
            jax.ShapeDtypeStruct((16, chans), F32),
        ),
        in_specs=[anywhere] * 4 + [inside] * 4,
        out_specs=(anywhere, anywhere, inside),
        scratch_shapes=[
            vm((rows + 2, cols, chans), BF16),
            vm(grid3, BF16),
            vm((chans, chans), BF16),
            vm((chans, chans), BF16),
            vm(grid3, F32),
            vm(grid3, BF16),
            vm(grid3, F32),
            vm(grid3, BF16),
            vm(grid3, BF16),
            vm((rows + 2, cols, chans), BF16),
            vm((16, cols, chans), F32),
            vm((rows, cols, 128), F32),
            vm((2, chans, chans), BF16),
            vm((2, chans // 2, chans), BF16),
            vm((4, pieces, chans), BF16),
            vm((2, chans, chans), BF16),
            vm((2, rows, chans), F32),
            vm((2, rows + 16, chans), F32),
            vm((2, rows, chans), F32),
            vm((4, rows, chans), BF16),
            vm((4, rows, chans), BF16),
            vm((4, 16, chans), BF16),
            vm((4, 16, chans), BF16),
            vm((cols, chans), F32),
            vm((cols, chans), F32),
            vm((bits + 1, 16, chans), F32),
            vm((bits, 16, chans), F32),
            dma((4,)),
            dma((12,)),
            dma((12,)),
            dma((2 + 4 * (bits - 1),)),
            dma((2 + 4 * (bits - 1),)),
            dma((4 * bits,)),
            dma((4 * bits,)),
            dma((bits,)),
            dma((bits,)),
        ],
        compiler_params=pltpu.CompilerParams(
            collective_id=0, has_side_effects=True, vmem_limit_bytes=62 * 1024 * 1024
        ),
    )(fields, cotangent, w_in, w_out, kernel, norm_gain[None], land_bias[None], land)
    wide = gw.astype(F32)
    return (out, wide[1], wide[0], small[:9], small[9], small[10])


def solution(mesh):
    placed = (
        P("groups", "tile", None),
        P(),
        P(),
        P(),
        P(),
        P(),
        P("groups", "tile"),
        P("groups", "tile", None),
    )
    return jax.shard_map(
        body,
        mesh=mesh,
        in_specs=placed,
        out_specs=(
            P("groups", "tile", None),
            P("groups", None),
            P("groups", None),
            P("groups", None),
            P("groups"),
            P("groups"),
        ),
        check_vma=False,
    )
```

```python
import functools

import jax
import jax.numpy as jnp
from jax import lax
from jax.experimental import pallas as pl
from jax.experimental.pallas import tpu as pltpu
from jax.sharding import PartitionSpec as P

EPS = 1e-06
INV_ROOT_TWO = 0.7071067811865476
INV_ROOT_TWO_PI = 0.3989422804014327
F32 = jnp.float32
BF16 = jnp.bfloat16
LANES = 256
NT = (((1,), (1,)), ((), ()))
TN = (((0,), (0,)), ((), ()))


def block_kernel(
    count, fields_hbm, cot_hbm, w_in_hbm, w_out_hbm, taps, gain, bias, land,
    out_hbm, gw_out_hbm, gw_in_hbm, small_out,
    F, COT, WI, WO, D, NRM, GH, HID, GP, GX, PRE, SC, SQ, G, RB, RP, A,
    COL, HX, EDGE, CS, CR, KS, KR, GA, LA, SS, SR,
    load_sem, halo_send, halo_recv, rs_send, rs_recv, ag_send, ag_recv, sm_send, sm_recv,
):
    rows, cols, chans = COT.shape
    me = lax.axis_index("tile")
    bits = count.bit_length() - 1
    half = count // 2
    right = (me + 1) % count
    left = (me + count - 1) % count
    across = (me + half) % count
    across_right = (me + half + 1) % count
    across_left = (me + half - 1) % count

    def bit_of(b):
        return (me // (1 << b)) % 2

    def peer(b):
        return me + (1 - 2 * bit_of(b)) * (1 << b)

    def remote(src, dst, send, recv, target):
        return pltpu.make_async_remote_copy(
            src_ref=src, dst_ref=dst, send_sem=send, recv_sem=recv,
            device_id={"tile": target}, device_id_type=pl.DeviceIdType.MESH,
        )

    load_f = pltpu.make_async_copy(fields_hbm, F.at[pl.ds(1, rows)], load_sem.at[0])
    load_c = pltpu.make_async_copy(cot_hbm, COT, load_sem.at[1])
    load_o = pltpu.make_async_copy(w_out_hbm, WO, load_sem.at[2])
    load_i = pltpu.make_async_copy(w_in_hbm, WI, load_sem.at[3])
    load_f.start()
    load_c.start()
    load_o.start()
    load_i.start()

    friends = [right, left, across, across_right, across_left] + [peer(b) for b in range(bits - 1)]
    barrier = pltpu.get_barrier_semaphore()
    for friend in friends:
        pl.semaphore_signal(barrier, inc=1, device_id={"tile": friend}, device_id_type=pl.DeviceIdType.MESH)
    pl.semaphore_wait(barrier, len(friends))

    lane_chunks = [pl.ds(c * LANES, LANES) for c in range(chans // LANES)]
    spot = lax.broadcasted_iota(jnp.int32, (cols, LANES), 0)
    first = spot == 0
    last = spot == cols - 1

    def send_halo(ext, base):
        copies = [
            remote(ext.at[1], ext.at[0], halo_send.at[base], halo_recv.at[base], across),
            remote(ext.at[rows], ext.at[rows + 1], halo_send.at[base + 1], halo_recv.at[base + 1], across),
        ]
        slot = 0 if base == 0 else 2
        for copy in copies:
            copy.start()
        for side in range(2):
            def rounded(t, _):
                at = pl.ds(pl.multiple_of(t * 16, 16), 16)
                CS[slot + side, at, :] = COL[side, at, :].astype(BF16)
                return 0
            lax.fori_loop(0, rows // 16, rounded, 0)
            ends = jnp.concatenate([COL[side, 0:8, :], COL[side, rows - 8 : rows, :]], axis=0)
            KS[slot + side] = ends.astype(BF16)
        more = [
            remote(CS.at[slot + 1], CR.at[slot], halo_send.at[base + 2], halo_recv.at[base + 2], right),
            remote(CS.at[slot], CR.at[slot + 1], halo_send.at[base + 3], halo_recv.at[base + 3], left),
            remote(KS.at[slot + 1], KR.at[slot], halo_send.at[base + 4], halo_recv.at[base + 4], across_right),
            remote(KS.at[slot], KR.at[slot + 1], halo_send.at[base + 5], halo_recv.at[base + 5], across_left),
        ]
        for copy in more:
            copy.start()
        return copies + more

    def widen_halo(slot):
        for side in range(2):
            def opened(t, _):
                at = pl.ds(pl.multiple_of(t * 16, 16), 16)
                HX[side, pl.ds(pl.multiple_of(8 + t * 16, 8), 16), :] = CR[slot + side, at, :].astype(F32)
                return 0
            lax.fori_loop(0, rows // 16, opened, 0)
            ends = KR[slot + side].astype(F32)
            HX[side, 7:8, :] = ends[0:1]
            HX[side, 8 + rows : 9 + rows, :] = ends[15:16]

    load_f.wait()

    def take_columns(i, _):
        row = F[i + 1].astype(F32)
        COL[0, pl.ds(i, 1), :] = row[0:1]
        COL[1, pl.ds(i, 1), :] = row[cols - 1 : cols]
        return 0
    lax.fori_loop(0, rows, take_columns, 0)
    halo = send_halo(F, 0)

    load_c.wait()
    load_o.wait()
    load_i.wait()
    step = 16
    blocks = rows // step

    def hidden_grad(k, _):
        at = pl.ds(k * step, step)
        up = COT[at].reshape(step * cols, chans)
        for lanes in lane_chunks:
            GH[at, :, lanes] = lax.dot_general(
                up, WO[lanes, :], NT, preferred_element_type=F32
            ).reshape(step, cols, LANES)
        return 0
    lax.fori_loop(0, blocks, hidden_grad, 0)

    for copy in halo:
        copy.wait()
    widen_halo(0)
    for lanes in lane_chunks:
        for side in range(2):
            total = taps[2 * side : 2 * side + 1, lanes] * HX[side, 7 : 7 + rows, lanes]
            for a in range(1, 3):
                t = 3 * a + 2 * side
                total = total + taps[t : t + 1, lanes] * HX[side, 7 + a : 7 + a + rows, lanes]
            EDGE[side, :, lanes] = total

    def forward(k, _):
        def depth_row(q, _):
            i = k * step + q
            squares = jnp.zeros((cols, 128), F32)
            ground = land[i]
            for lanes in lane_chunks:
                window = [F[i + a, :, lanes].astype(F32) for a in range(3)]
                sums = []
                for b in range(3):
                    s = taps[b : b + 1, lanes] * window[0]
                    for a in range(1, 3):
                        s = s + taps[3 * a + b : 3 * a + b + 1, lanes] * window[a]
                    sums.append(s)
                depth = sums[1]
                depth = depth + jnp.where(first, EDGE[0, pl.ds(i, 1), lanes], pltpu.roll(sums[0], 1, 0))
                depth = depth + jnp.where(last, EDGE[1, pl.ds(i, 1), lanes], pltpu.roll(sums[2], cols - 1, 0))
                depth = depth + jnp.concatenate([ground] * (LANES // 128), axis=1) * bias[0:1, lanes]
                D[i, :, lanes] = depth
                for part in range(LANES // 128):
                    piece = depth[:, part * 128 : (part + 1) * 128]
                    squares = squares + piece * piece
            SQ[q] = squares
            return 0
        lax.fori_loop(0, step, depth_row, 0, unroll=2)
        mean = jnp.sum(SQ[...], axis=2, keepdims=True) * (1.0 / chans)
        SC[pl.ds(k * step, step)] = jnp.broadcast_to(lax.rsqrt(mean + EPS), (step, cols, 128))

        def norm_row(q, _):
            i = k * step + q
            wide = jnp.concatenate([SC[i]] * (LANES // 128), axis=1)
            for lanes in lane_chunks:
                NRM[i, :, lanes] = (D[i, :, lanes] * wide * gain[0:1, lanes]).astype(BF16)
            return 0
        lax.fori_loop(0, step, norm_row, 0, unroll=2)
        normed = NRM[pl.ds(k * step, step)].reshape(step * cols, chans)
        for lanes in lane_chunks:
            PRE[:, :, lanes] = jnp.dot(
                normed, WI[:, lanes], preferred_element_type=F32
            ).reshape(step, cols, LANES)

        def gelu_row(q, _):
            i = k * step + q
            for lanes in lane_chunks:
                pre = PRE[q, :, lanes]
                cdf = 0.5 * (1.0 + lax.erf(pre * INV_ROOT_TWO))
                slope = cdf + pre * jnp.exp(-0.5 * pre * pre) * INV_ROOT_TWO_PI
                HID[i, :, lanes] = (pre * cdf).astype(BF16)
                GP[i, :, lanes] = (GH[i, :, lanes] * slope).astype(BF16)
            return 0
        lax.fori_loop(0, step, gelu_row, 0, unroll=2)
        return 0
    lax.fori_loop(0, blocks, forward, 0)

    core = bit_of(0)
    mid = chans // 2
    keep0 = pl.multiple_of(core * mid, mid)
    send0 = pl.multiple_of((1 - core) * mid, mid)

    def weight_grad(w, lhs, rhs, base):
        def chunk(t, _):
            at = pl.ds(pl.multiple_of(base + t * LANES, LANES), LANES)
            left_side = lhs[:, :, at].reshape(rows * cols, LANES)
            for lanes in lane_chunks:
                right_side = rhs[:, :, lanes].reshape(rows * cols, LANES)
                G[w, at, lanes] = lax.dot_general(
                    left_side, right_side, TN, preferred_element_type=F32
                ).astype(BF16)
            return 0
        lax.fori_loop(0, mid // LANES, chunk, 0)

    def swap_core(w):
        copy = remote(G.at[w, pl.ds(send0, mid)], RB.at[w], rs_send.at[w], rs_recv.at[w], peer(0))
        copy.start()
        return copy

    def fold(w, base, size, source, offset):
        def add(t, _):
            at = pl.ds(pl.multiple_of(base + t * 16, 16), 16)
            come = source[pl.ds(pl.multiple_of(offset + t * 16, 16), 16), :]
            G[w, at, :] = (G[w, at, :].astype(F32) + come.astype(F32)).astype(BF16)
            return 0
        lax.fori_loop(0, size // 16, add, 0)

    middle = list(range(1, bits - 1))
    pieces = mid // 2
    orders = []
    bases = []
    for p in range(4):
        turn = p % len(middle)
        orders.append(middle[turn:] + middle[:turn] + [bits - 1])
        bases.append([keep0 + (p % 2) * pieces])
    stages = bits - 1
    offsets = [pieces - (pieces >> s) for s in range(stages)]

    def rs_start(p, s):
        size = pieces >> (s + 1)
        b = orders[p][s]
        base = bases[p][s]
        away = pl.multiple_of(base + (1 - bit_of(b)) * size, 16)
        bases[p].append(base + bit_of(b) * size)
        n = 2 + p * stages + s
        copy = remote(
            G.at[p // 2, pl.ds(away, size)], RP.at[p, pl.ds(offsets[s], size)],
            rs_send.at[n], rs_recv.at[n], peer(b),
        )
        copy.start()
        return copy

    def rs_finish(copy, p, s):
        copy.wait()
        fold(p // 2, bases[p][s + 1], pieces >> (s + 1), RP.at[p], offsets[s])

    def ag_start(p, s):
        size = pieces >> (s + 1)
        at = pl.ds(pl.multiple_of(bases[p][s + 1], 16), size)
        b = orders[p][s] if s >= 0 else 0
        n = p * bits + s + 1
        copy = remote(A.at[p // 2, at], A.at[p // 2, at], ag_send.at[n], ag_recv.at[n], peer(b))
        copy.start()
        return copy

    flight = {}

    def advance(p):
        state, copy = flight[p]
        if state[0] == "rs":
            s = state[1]
            rs_finish(copy, p, s)
            if s + 1 < stages:
                flight[p] = (("rs", s + 1), rs_start(p, s + 1))
            else:
                at = pl.ds(pl.multiple_of(bases[p][stages], 16), pieces >> stages)
                A[p // 2, at, :] = G[p // 2, at, :]
                flight[p] = (("ag", stages - 1), ag_start(p, stages - 1))
        elif state[0] == "ag":
            s = state[1]
            copy.wait()
            if s >= 0:
                flight[p] = (("ag", s - 1), ag_start(p, s - 1))
            else:
                flight[p] = (("done",), None)

    weight_grad(0, HID, COT, send0)
    core0 = swap_core(0)
    weight_grad(0, HID, COT, keep0)
    core0.wait()
    fold(0, keep0, mid, RB.at[0], 0)
    for p in (0, 1):
        flight[p] = (("rs", 0), rs_start(p, 0))
    weight_grad(1, NRM, GP, send0)
    core1 = swap_core(1)
    weight_grad(1, NRM, GP, keep0)
    core1.wait()
    fold(1, keep0, mid, RB.at[1], 0)
    for p in (2, 3):
        flight[p] = (("rs", 0), rs_start(p, 0))
    for p in (0, 1):
        advance(p)

    GA[...] = jnp.zeros_like(GA)
    LA[...] = jnp.zeros_like(LA)

    def backward(k, _):
        at = pl.ds(k * step, step)
        g_pre = GP[at].reshape(step * cols, chans)
        for lanes in lane_chunks:
            GH[at, :, lanes] = lax.dot_general(
                g_pre, WI[lanes, :], NT, preferred_element_type=F32
            ).reshape(step, cols, LANES)

        def inner_row(q, _):
            i = k * step + q
            wide = jnp.concatenate([SC[i]] * (LANES // 128), axis=1)
            inner = jnp.zeros((cols, 128), F32)
            for lanes in lane_chunks:
                g = GH[i, :, lanes]
                product = g * D[i, :, lanes]
                GA[:, lanes] = GA[:, lanes] + product * wide
                weighted = product * gain[0:1, lanes]
                for part in range(LANES // 128):
                    inner = inner + weighted[:, part * 128 : (part + 1) * 128]
            SQ[q] = inner
            return 0
        lax.fori_loop(0, step, inner_row, 0, unroll=2)
        mean = jnp.sum(SQ[...], axis=2, keepdims=True) * (1.0 / chans)
        scales = SC[at]
        SQ[...] = scales * scales * scales * mean

        def depth_grad_row(q, _):
            i = k * step + q
            wide = jnp.concatenate([SC[i]] * (LANES // 128), axis=1)
            cube = jnp.concatenate([SQ[q]] * (LANES // 128), axis=1)
            ground = jnp.concatenate([land[i]] * (LANES // 128), axis=1)
            for lanes in lane_chunks:
                g = wide * (GH[i, :, lanes] * gain[0:1, lanes]) - D[i, :, lanes] * cube
                rounded = g.astype(BF16)
                GX[i + 1, :, lanes] = rounded
                g = rounded.astype(F32)
                LA[:, lanes] = LA[:, lanes] + g * ground
                COL[0, pl.ds(i, 1), lanes] = g[0:1]
                COL[1, pl.ds(i, 1), lanes] = g[cols - 1 : cols]
            return 0
        lax.fori_loop(0, step, depth_grad_row, 0, unroll=2)
        return 0

    cuts = [blocks * t // 3 for t in range(4)]
    lax.fori_loop(cuts[0], cuts[1], backward, 0)
    for p in range(4):
        advance(p)
    lax.fori_loop(cuts[1], cuts[2], backward, 0)
    for p in range(4):
        advance(p)
    lax.fori_loop(cuts[2], cuts[3], backward, 0)
    g_halo = send_halo(GX, 6)
    for p in range(4):
        advance(p)

    zero = jnp.zeros((8, LANES), F32)
    for c, lanes in enumerate(lane_chunks):
        def tap_row(i, sums):
            g = GX[i + 1, :, lanes].astype(F32)
            sides = [
                jnp.where(last, 0.0, pltpu.roll(g, cols - 1, 0)),
                g,
                jnp.where(first, 0.0, pltpu.roll(g, 1, 0)),
            ]
            new = []
            for a in range(3):
                row = F[i + a, :, lanes].astype(F32)
                for b in range(3):
                    product = sides[b] * row
                    piece = product[0:8]
                    for top in range(8, cols, 8):
                        piece = piece + product[top : top + 8]
                    new.append(sums[3 * a + b] + piece)
            return tuple(new)
        sums = list(lax.fori_loop(0, rows, tap_row, (zero,) * 9, unroll=2))
        lines = []
        for a in range(3):
            for b in range(3):
                line = jnp.sum(sums[3 * a + b], axis=0, keepdims=True)
                if b != 1:
                    side = b // 2
                    line = line + jnp.sum(
                        COL[side, :, lanes] * HX[side, 7 + a : 7 + a + rows, lanes], axis=0, keepdims=True
                    )
                lines.append(line)
        lines.append(jnp.sum(GA[:, lanes], axis=0, keepdims=True))
        lines.append(jnp.sum(LA[:, lanes], axis=0, keepdims=True))
        lines.append(jnp.zeros((5, LANES), F32))
        SS[0, :, lanes] = jnp.concatenate(lines, axis=0)
        if c % 2 == 1:
            for p in range(4):
                advance(p)

    def small_start(b):
        copy = remote(SS.at[b], SR.at[b], sm_send.at[b], sm_recv.at[b], peer(b))
        copy.start()
        return copy

    def small_finish(copy, b):
        copy.wait()
        SS[b + 1] = SS[b] + SR[b]

    small = small_start(0)
    for copy in g_halo:
        copy.wait()
    widen_halo(2)
    for lanes in lane_chunks:
        for side in range(2):
            north = HX[side, 7:8, lanes]
            south = HX[side, 8 + rows : 9 + rows, lanes]
            near = 2 - 2 * side
            middle_rows = taps[3 + near : 4 + near, lanes] * HX[side, 8 : 8 + rows, lanes]
            above = taps[6 + near : 7 + near, lanes] * HX[side, 7 : 7 + rows, lanes]
            below = taps[near : near + 1, lanes] * HX[side, 9 : 9 + rows, lanes]
            line = lax.broadcasted_iota(jnp.int32, (rows, LANES), 0)
            above = jnp.where(line == 0, taps[near : near + 1, lanes] * north, above)
            below = jnp.where(line == rows - 1, taps[6 + near : 7 + near, lanes] * south, below)
            EDGE[side, :, lanes] = middle_rows + above + below

    def spread_row(i, top, bottom):
        for lanes in lane_chunks:
            above = GX[i, :, lanes].astype(F32)
            here = GX[i + 1, :, lanes].astype(F32)
            below = GX[i + 2, :, lanes].astype(F32)
            sums = []
            for b in range(3):
                s = taps[3 * top + b : 3 * top + b + 1, lanes] * above
                s = s + taps[3 + b : 4 + b, lanes] * here
                s = s + taps[3 * bottom + b : 3 * bottom + b + 1, lanes] * below
                sums.append(s)
            total = sums[1] + COT[i, :, lanes].astype(F32)
            total = total + jnp.where(last, EDGE[1, pl.ds(i, 1), lanes], pltpu.roll(sums[0], cols - 1, 0))
            total = total + jnp.where(first, EDGE[0, pl.ds(i, 1), lanes], pltpu.roll(sums[2], 1, 0))
            HID[i, :, lanes] = total.astype(BF16)

    def spread(i, _):
        spread_row(i, 2, 0)
        return 0

    spread_row(0, 0, 0)
    spread_row(rows - 1, 2, 2)
    legs = bits
    edges = [1 + (rows - 2) * t // legs for t in range(legs + 1)]
    for t in range(legs):
        lax.fori_loop(edges[t], edges[t + 1], spread, 0)
        small_finish(small, t)
        if t + 1 < bits:
            small = small_start(t + 1)
        for p in range(4):
            advance(p)
    store = pltpu.make_async_copy(HID, out_hbm, load_sem.at[0])
    store.start()
    for _ in range(2 * bits):
        for p in range(4):
            advance(p)
    small_out[...] = SS[bits]
    save_out = pltpu.make_async_copy(A.at[0], gw_out_hbm, load_sem.at[1])
    save_in = pltpu.make_async_copy(A.at[1], gw_in_hbm, load_sem.at[2])
    save_out.start()
    save_in.start()
    store.wait()
    save_out.wait()
    save_in.wait()


def body(fields, kernel, norm_gain, land_bias, w_in, w_out, land_mask, cotangent):
    rows, cols, chans = fields.shape
    count = lax.axis_size("tile")
    bits = count.bit_length() - 1
    land = jnp.broadcast_to(land_mask.astype(F32)[:, :, None], (rows, cols, 128))
    vm = pltpu.VMEM
    grid3 = (rows, cols, chans)
    dma = pltpu.SemaphoreType.DMA
    anywhere = pl.BlockSpec(memory_space=pl.ANY)
    inside = pl.BlockSpec(memory_space=pltpu.VMEM)
    pieces = chans // 4
    out, gw_out, gw_in, small = pl.pallas_call(
        functools.partial(block_kernel, count),
        out_shape=(
            jax.ShapeDtypeStruct(grid3, BF16),
            jax.ShapeDtypeStruct((chans, chans), BF16),
            jax.ShapeDtypeStruct((chans, chans), BF16),
            jax.ShapeDtypeStruct((16, chans), F32),
        ),
        in_specs=[anywhere] * 4 + [inside] * 4,
        out_specs=(anywhere, anywhere, anywhere, inside),
        scratch_shapes=[
            vm((rows + 2, cols, chans), BF16),
            vm(grid3, BF16),
            vm((chans, chans), BF16),
            vm((chans, chans), BF16),
            vm(grid3, F32),
            vm(grid3, BF16),
            vm(grid3, F32),
            vm(grid3, BF16),
            vm(grid3, BF16),
            vm((rows + 2, cols, chans), BF16),
            vm((16, cols, chans), F32),
            vm((rows, cols, 128), F32),
            vm((16, cols, 128), F32),
            vm((2, chans, chans), BF16),
            vm((2, chans // 2, chans), BF16),
            vm((4, pieces, chans), BF16),
            vm((2, chans, chans), BF16),
            vm((2, rows, chans), F32),
            vm((2, rows + 16, chans), F32),
            vm((2, rows, chans), F32),
            vm((4, rows, chans), BF16),
            vm((4, rows, chans), BF16),
            vm((4, 16, chans), BF16),
            vm((4, 16, chans), BF16),
            vm((cols, chans), F32),
            vm((cols, chans), F32),
            vm((bits + 1, 16, chans), F32),
            vm((bits, 16, chans), F32),
            dma((4,)),
            dma((12,)),
            dma((12,)),
            dma((2 + 4 * (bits - 1),)),
            dma((2 + 4 * (bits - 1),)),
            dma((4 * bits,)),
            dma((4 * bits,)),
            dma((bits,)),
            dma((bits,)),
        ],
        compiler_params=pltpu.CompilerParams(
            collective_id=0, has_side_effects=True, vmem_limit_bytes=62 * 1024 * 1024
        ),
    )(fields, cotangent, w_in, w_out, kernel, norm_gain[None], land_bias[None], land)
    return (out, gw_in.astype(F32), gw_out.astype(F32), small[:9], small[9], small[10])


def solution(mesh):
    placed = (
        P("groups", "tile", None),
        P(),
        P(),
        P(),
        P(),
        P(),
        P("groups", "tile"),
        P("groups", "tile", None),
    )
    return jax.shard_map(
        body,
        mesh=mesh,
        in_specs=placed,
        out_specs=(
            P("groups", "tile", None),
            P("groups", None),
            P("groups", None),
            P("groups", None),
            P("groups"),
            P("groups"),
        ),
        check_vma=False,
    )
```
